32 devices in a mesh: lat: 4 (over x, core), lon: 4 (over z), ch: 2 (over y).
Axes of the slice: x: 2, y: 2, z: 4, core: 2. Of those that a mesh axis runs over, the one named last changes fastest.
Arguments:
- grid_tokens: bfloat16 [1, 256, 768, 768], P(None, 'lat', 'lon'), may hold values from -6 to 6
- first_gain: float32 [768], replicated, may hold values from 0.1 to 1.9
- first_bias: float32 [768], replicated, may hold values from -3 to 3
- first_filter: bfloat16 [2, 8, 96, 96], P(None, 'ch'), may hold values from -0.4375 to 0.4375
- first_shift: float32 [2, 8, 96], P(None, 'ch'), may hold values from -3 to 3
- second_filter: bfloat16 [2, 8, 96, 96], P(None, 'ch'), may hold values from -0.4375 to 0.4375
- second_shift: float32 [2, 8, 96], P(None, 'ch'), may hold values from -3 to 3
- mode_mask: int32 [256, 384], P(None, ('lat', 'lon')), may hold values 0 or 1
- second_gain: float32 [768], replicated, may hold values from 0.1 to 1.9
- second_bias: float32 [768], replicated, may hold values from -3 to 3
- up_weight: bfloat16 [768, 3072], P(None, 'ch'), may hold values from -0.21875 to 0.21875
- up_bias: float32 [3072], P('ch'), may hold values from -3 to 3
- down_weight: bfloat16 [3072, 768], P('ch'), may hold values from -0.109375 to 0.109375
- down_bias: float32 [768], P('ch'), may hold values from -3 to 3
Outputs:
- block_output: bfloat16 [1, 256, 768, 768], P(None, ('lat', 'lon'), None, 'ch')
The draws below stay inside these ranges and needn't reach their ends.
Inputs may be any that keep to these rules, and one draw needn't show every extreme that they name: `mode_mask`: 1 keeps a mode, 0 drops it.
All inputs are finite; a program needn't handle non-finite values. No bound on the sum of `mode_mask` on one device may be relied on, other than what follows from the above.
Results may differ from the reference program's by a relative error of at most 0.009.
Values may be sent and summed in bfloat16 or wider, within the bound.
A program may use at most 192 MiB of HBM per device.

```python
import math
import jax
import jax.numpy as jnp
from jax import lax

SAMPLES = 1
LAT_ROWS = 256
LON_COLS = 768
LON_MODES = 384
CHANNELS = 768
BLOCKS = 8
BLOCK_SIZE = 96
HIDDEN_SIZE = 3072
N_CH = 2


def set_ends(entries, rng, low, high):
    shape = entries.shape
    place = [jax.random.randint(jax.random.fold_in(rng, axis), (), 0, shape[axis]) for axis in range(len(shape))]
    entries = entries.at[tuple(place)].set(low)
    longest = shape.index(max(shape))
    place[longest] = (place[longest] + 1) % shape[longest]
    return entries.at[tuple(place)].set(high)


def levels(own_key, dims, shards, low, top_value):
    level = 1.0
    for axis_at, parts in shards:
        draws = jax.random.uniform(jax.random.fold_in(jax.random.fold_in(own_key, 6), axis_at), (parts,), jnp.float32, low / len(shards), top_value / len(shards))
        level = level * jnp.repeat(jnp.exp(draws), dims[axis_at] // parts).reshape((-1,) + (1,) * (len(dims) - 1 - axis_at))
    return level


def bell_draw(stream_key, shape, width, limit, pieces=(), kind=jnp.bfloat16):
    factor_of = levels(stream_key, shape, pieces, -0.22, 0.18) if pieces else 1.0
    values = jax.random.normal(stream_key, shape, jnp.float32) * width * factor_of
    return jnp.minimum(jnp.maximum(values, -limit), limit).astype(kind)


def setup_inputs(seed: int = 0) -> dict:
    key_list = jax.random.split(jax.random.key(seed), 15)
    return {
        "grid_tokens": bell_draw(key_list[0], (SAMPLES, LAT_ROWS, LON_COLS, CHANNELS), 1.0, 6.0, ((1, 4), (2, 4))),
        "first_gain": jnp.clip(1.0 + 0.18 * jax.random.normal(key_list[1], (CHANNELS,), jnp.float32), 0.1, 1.9),
        "first_bias": bell_draw(key_list[2], (CHANNELS,), 0.5, 3.0, (), jnp.float32),
        "first_filter": bell_draw(key_list[3], (2, BLOCKS, BLOCK_SIZE, BLOCK_SIZE), (2 * BLOCK_SIZE) ** -0.5, 0.4375, ((1, 2),)),
        "first_shift": bell_draw(key_list[4], (2, BLOCKS, BLOCK_SIZE), 0.5, 3.0, ((1, 2),), jnp.float32),
        "second_filter": bell_draw(key_list[5], (2, BLOCKS, BLOCK_SIZE, BLOCK_SIZE), (2 * BLOCK_SIZE) ** -0.5, 0.4375, ((1, 2),)),
        "second_shift": bell_draw(key_list[6], (2, BLOCKS, BLOCK_SIZE), 0.5, 3.0, ((1, 2),), jnp.float32),
        "mode_mask": set_ends((jax.random.randint(key_list[7], (LAT_ROWS, LON_MODES), 0, 4) < 3).astype(jnp.int32), jax.random.fold_in(key_list[7], 1), 0, 1),
        "second_gain": jnp.clip(1.0 + 0.18 * jax.random.normal(key_list[8], (CHANNELS,), jnp.float32), 0.1, 1.9),
        "second_bias": bell_draw(key_list[9], (CHANNELS,), 0.5, 3.0, (), jnp.float32),
        "up_weight": bell_draw(key_list[10], (CHANNELS, HIDDEN_SIZE), CHANNELS ** -0.5, 0.21875, ((1, 2),)),
        "up_bias": bell_draw(key_list[11], (HIDDEN_SIZE,), 0.5, 3.0, ((0, 2),), jnp.float32),
        "down_weight": bell_draw(key_list[12], (HIDDEN_SIZE, CHANNELS), HIDDEN_SIZE ** -0.5, 0.109375, ((0, 2),)),
        "down_bias": bell_draw(key_list[13], (CHANNELS,), 0.5, 3.0, ((0, 2),), jnp.float32),
    }


shrink_level = 0.01
norm_epsilon = 1e-05

def layer_norm(values, gain_vector, shift_vector):
    values = values.astype(jnp.float32)
    center = lax.optimization_barrier(jnp.mean(values, axis=-1, keepdims=True))
    spread = lax.optimization_barrier(jnp.mean(jnp.square(values - center), axis=-1, keepdims=True))
    return (values - center) * lax.rsqrt(spread + norm_epsilon) * gain_vector + shift_vector

def lon_tables(lon_width, mode_count):
    frequency = jnp.arange(mode_count, dtype=jnp.int32)[:, None]
    position = jnp.arange(lon_width, dtype=jnp.int32)[None, :]
    phases = frequency * position % lon_width
    angles = phases.astype(jnp.float32) * (2.0 * math.pi / lon_width)
    norm_scale = 1.0 / math.sqrt(lon_width)
    forward = jnp.stack([jnp.cos(angles) * norm_scale, -jnp.sin(angles) * norm_scale]).astype(jnp.bfloat16)
    factor = jnp.where(frequency == 0, 1.0, 2.0) * norm_scale
    inverse = jnp.stack([jnp.cos(angles) * factor, -jnp.sin(angles) * factor]).astype(jnp.bfloat16)
    return (forward, inverse)

def lat_tables(lat_height):
    indices = jnp.arange(lat_height, dtype=jnp.int32)
    phases = indices[:, None] * indices[None, :] % lat_height
    angles = phases.astype(jnp.float32) * (2.0 * math.pi / lat_height)
    norm_scale = 1.0 / math.sqrt(lat_height)
    cosine = jnp.cos(angles) * norm_scale
    sine_table = jnp.sin(angles) * norm_scale
    forward = jnp.stack([jnp.stack([cosine, sine_table]), jnp.stack([-sine_table, cosine])]).astype(jnp.bfloat16)
    inverse = jnp.stack([jnp.stack([cosine, -sine_table]), jnp.stack([sine_table, cosine])]).astype(jnp.bfloat16)
    return (forward, inverse)

def complex_weight(weights):
    real_part, imag_part = (weights[0], weights[1])
    top_half = jnp.stack([real_part, imag_part], axis=2)
    low_half = jnp.stack([-imag_part, real_part], axis=2)
    return jnp.stack([top_half, low_half])

def mode_mixer(spectrum, weight_one, shift_one, weight_two, shift_two, keep_mask):
    samples, _, lat_freqs, lon_freqs, channel_count = spectrum.shape
    block_count = weight_one.shape[1]
    block_width = weight_one.shape[2]
    split_spec = spectrum.reshape(samples, 2, lat_freqs, lon_freqs, block_count, block_width).astype(jnp.float32)
    first_layer = jnp.einsum('bpxyni,pniqo->bqxyno', split_spec, complex_weight(weight_one).astype(jnp.float32))
    first_layer = jnp.maximum(first_layer + shift_one[None, :, None, None, :, :], 0.0).astype(jnp.bfloat16)
    second_layer = jnp.einsum('bpxyni,pniqo->bqxyno', first_layer.astype(jnp.float32), complex_weight(weight_two).astype(jnp.float32))
    second_layer = second_layer + shift_two[None, :, None, None, :, :]
    second_layer = second_layer - jnp.clip(second_layer, -shrink_level, shrink_level)
    second_layer = second_layer * keep_mask.astype(jnp.float32)[None, None, :, :, None, None]
    return second_layer.astype(jnp.bfloat16).reshape(samples, 2, lat_freqs, lon_freqs, channel_count)

def reference(grid_tokens, first_gain, first_bias, first_filter, first_shift, second_filter, second_shift, mode_mask, second_gain, second_bias, up_weight, up_bias, down_weight, down_bias):
    normed = layer_norm(grid_tokens, first_gain, first_bias).astype(jnp.bfloat16)
    lon_forward, lon_inverse = lon_tables(LON_COLS, LON_MODES)
    lat_forward, lat_inverse = lat_tables(LAT_ROWS)
    row_spectrum = jnp.einsum('pkw,bhwc->bhpkc', lon_forward.astype(jnp.float32), normed.astype(jnp.float32)).astype(jnp.bfloat16)
    spectrum = jnp.einsum('qpxh,bhpyc->bqxyc', lat_forward.astype(jnp.float32), row_spectrum.astype(jnp.float32)).astype(jnp.bfloat16)
    filtered_modes = mode_mixer(spectrum, first_filter, first_shift, second_filter, second_shift, mode_mask)
    row_modes = jnp.einsum('qphx,bpxyc->bhqyc', lat_inverse.astype(jnp.float32), filtered_modes.astype(jnp.float32)).astype(jnp.bfloat16)
    filtered = jnp.einsum('pkw,bhpkc->bhwc', lon_inverse.astype(jnp.float32), row_modes.astype(jnp.float32))
    mixed = (grid_tokens.astype(jnp.float32) + normed.astype(jnp.float32) + filtered).astype(jnp.bfloat16)
    group_width = HIDDEN_SIZE // N_CH
    down_groups = down_weight.reshape(N_CH, group_width, CHANNELS).astype(jnp.float32)

    def feed_forward(row_slab):
        normed_two = layer_norm(row_slab, second_gain, second_bias).astype(jnp.bfloat16)
        tokens = normed_two.reshape(-1, CHANNELS)
        hidden = jnp.dot(tokens, up_weight, preferred_element_type=jnp.float32) + up_bias
        hidden = jax.nn.gelu(hidden, approximate=False).astype(jnp.bfloat16)
        grouped = hidden.reshape(-1, N_CH, group_width).astype(jnp.float32)
        partials = jnp.einsum('tgj,gjc->tgc', grouped, down_groups).astype(jnp.bfloat16)
        total_sum = lax.optimization_barrier(jnp.sum(partials.astype(jnp.float32), axis=1)) + down_bias + row_slab.reshape(-1, CHANNELS).astype(jnp.float32)
        return total_sum.astype(jnp.bfloat16).reshape(row_slab.shape)
    results = lax.map(feed_forward, jnp.swapaxes(mixed, 0, 1))
    return jnp.swapaxes(results, 0, 1)
```

```python
import math

import jax
import jax.numpy as jnp
from jax import lax
from jax.sharding import PartitionSpec as P

shrink_level = 0.01
norm_epsilon = 1e-05
step_limit = 4
block_total = 8


def lon_tables(lon_width, mode_count):
    frequency = jnp.arange(mode_count, dtype=jnp.int32)[:, None]
    position = jnp.arange(lon_width, dtype=jnp.int32)[None, :]
    phases = frequency * position % lon_width
    angles = phases.astype(jnp.float32) * (2.0 * math.pi / lon_width)
    norm_scale = 1.0 / math.sqrt(lon_width)
    forward = jnp.stack([jnp.cos(angles) * norm_scale, -jnp.sin(angles) * norm_scale]).astype(
        jnp.bfloat16
    )
    factor = jnp.where(frequency == 0, 1.0, 2.0) * norm_scale
    inverse = jnp.stack([jnp.cos(angles) * factor, -jnp.sin(angles) * factor]).astype(jnp.bfloat16)
    return (forward, inverse)


def lat_tables(lat_height):
    indices = jnp.arange(lat_height, dtype=jnp.int32)
    phases = indices[:, None] * indices[None, :] % lat_height
    angles = phases.astype(jnp.float32) * (2.0 * math.pi / lat_height)
    norm_scale = 1.0 / math.sqrt(lat_height)
    cosine = jnp.cos(angles) * norm_scale
    sine_table = jnp.sin(angles) * norm_scale
    forward = jnp.stack([jnp.stack([cosine, sine_table]), jnp.stack([-sine_table, cosine])]).astype(
        jnp.bfloat16
    )
    inverse = jnp.stack([jnp.stack([cosine, -sine_table]), jnp.stack([sine_table, cosine])]).astype(
        jnp.bfloat16
    )
    return (forward, inverse)


def complex_weight(weights):
    real_part, imag_part = (weights[0], weights[1])
    top_half = jnp.stack([real_part, imag_part], axis=2)
    low_half = jnp.stack([-imag_part, real_part], axis=2)
    return jnp.stack([top_half, low_half])


def mode_mixer(spectrum, weight_one, shift_one, weight_two, shift_two, keep_mask):
    samples, _, lat_freqs, lon_freqs, channel_count = spectrum.shape
    block_count = weight_one.shape[1]
    block_width = weight_one.shape[2]
    split_spec = spectrum.reshape(samples, 2, lat_freqs, lon_freqs, block_count, block_width)
    first_layer = jnp.einsum(
        "bpxyni,pniqo->bqxyno",
        split_spec,
        complex_weight(weight_one),
        preferred_element_type=jnp.float32,
    )
    first_layer = jnp.maximum(first_layer + shift_one[None, :, None, None, :, :], 0.0).astype(
        jnp.bfloat16
    )
    second_layer = jnp.einsum(
        "bpxyni,pniqo->bqxyno",
        first_layer,
        complex_weight(weight_two),
        preferred_element_type=jnp.float32,
    )
    second_layer = second_layer + shift_two[None, :, None, None, :, :]
    second_layer = second_layer - jnp.clip(second_layer, -shrink_level, shrink_level)
    second_layer = second_layer * keep_mask.astype(jnp.float32)[None, None, :, :, None, None]
    return second_layer.astype(jnp.bfloat16).reshape(
        samples, 2, lat_freqs, lon_freqs, channel_count
    )


def dense_shards(
    grid_tokens,
    first_gain,
    first_bias,
    first_filter,
    first_shift,
    second_filter,
    second_shift,
    mode_mask,
    second_gain,
    second_bias,
    up_weight,
    up_bias,
    down_weight,
    down_bias,
):
    lat_count = lax.axis_size("lat")
    lon_count = lax.axis_size("lon")
    ch_count = lax.axis_size("ch")
    samples, rows_here, cols_here, channel_count = grid_tokens.shape
    full_width = cols_here * lon_count
    full_height = rows_here * lat_count
    part_chans = channel_count // ch_count
    offset = lax.axis_index("ch") * part_chans
    spread_count = lat_count * lon_count
    modes_here = full_width // 2 // spread_count
    values = grid_tokens.astype(jnp.float32)
    center = jnp.mean(values, axis=-1, keepdims=True)
    inv_dev = lax.rsqrt(
        jnp.mean(jnp.square(values - center), axis=-1, keepdims=True) + norm_epsilon
    )
    token_part = lax.dynamic_slice_in_dim(grid_tokens, offset, part_chans, 3)
    gain_part = lax.dynamic_slice_in_dim(first_gain, offset, part_chans, 0)
    bias_part = lax.dynamic_slice_in_dim(first_bias, offset, part_chans, 0)
    token_rows = lax.all_to_all(token_part, "lon", split_axis=1, concat_axis=2, tiled=True)
    moments = lax.all_to_all(
        jnp.concatenate([center, inv_dev], axis=3), "lon", split_axis=1, concat_axis=2, tiled=True
    )
    normed_rows = (
        (token_rows.astype(jnp.float32) - moments[..., 0:1]) * moments[..., 1:2] * gain_part
        + bias_part
    ).astype(jnp.bfloat16)
    row_pairs = normed_rows.shape[1]
    lon_forward, lon_inverse = lon_tables(full_width, full_width // 2)
    lat_forward, lat_inverse = lat_tables(full_height)
    row_spectrum = jnp.einsum(
        "pkw,brwc->brpkc", lon_forward, normed_rows, preferred_element_type=jnp.float32
    ).astype(jnp.bfloat16)
    packed = row_spectrum.reshape(samples, 1, row_pairs, 2, spread_count, modes_here, part_chans)
    arrived = lax.all_to_all(packed, ("lat", "lon"), split_axis=4, concat_axis=1, tiled=True)
    spectrum_rows = arrived.reshape(samples, full_height, 2, modes_here, part_chans)
    spectrum = jnp.einsum(
        "qpxh,bhpyc->bqxyc", lat_forward, spectrum_rows, preferred_element_type=jnp.float32
    ).astype(jnp.bfloat16)
    filtered_modes = mode_mixer(
        spectrum, first_filter, first_shift, second_filter, second_shift, mode_mask
    )
    back_rows = jnp.einsum(
        "qphx,bpxyc->bhqyc", lat_inverse, filtered_modes, preferred_element_type=jnp.float32
    ).astype(jnp.bfloat16)
    packed_back = back_rows.reshape(samples, spread_count, row_pairs, 2, 1, modes_here, part_chans)
    returned = lax.all_to_all(packed_back, ("lat", "lon"), split_axis=1, concat_axis=4, tiled=True)
    row_modes = returned.reshape(samples, row_pairs, 2, full_width // 2, part_chans)
    filtered = jnp.einsum(
        "pkw,brpkc->brwc", lon_inverse, row_modes, preferred_element_type=jnp.float32
    )
    mixed = (token_rows.astype(jnp.float32) + normed_rows.astype(jnp.float32) + filtered).astype(
        jnp.bfloat16
    )
    all_channels = lax.all_gather(mixed, "ch", axis=3, tiled=True).astype(jnp.float32)
    center_two = jnp.mean(all_channels, axis=-1, keepdims=True)
    inv_two = lax.rsqrt(
        jnp.mean(jnp.square(all_channels - center_two), axis=-1, keepdims=True) + norm_epsilon
    )
    normed_two = ((all_channels - center_two) * inv_two * second_gain + second_bias).astype(
        jnp.bfloat16
    )
    tokens = normed_two.reshape(-1, channel_count)
    hidden = jnp.dot(tokens, up_weight, preferred_element_type=jnp.float32) + up_bias
    hidden = jax.nn.gelu(hidden, approximate=False).astype(jnp.bfloat16)
    partial_rows = jnp.dot(hidden, down_weight, preferred_element_type=jnp.float32).reshape(
        samples, row_pairs, full_width, channel_count
    )
    summed = lax.psum_scatter(
        partial_rows.astype(jnp.bfloat16), "ch", scatter_dimension=3, tiled=True
    ).astype(jnp.float32)
    return (mixed.astype(jnp.float32) + down_bias + summed).astype(jnp.bfloat16)


def gelu(values):
    return 0.5 * values * (1.0 + lax.erf(values * math.sqrt(0.5)))


def block_shards(
    grid_tokens,
    first_gain,
    first_bias,
    first_filter,
    first_shift,
    second_filter,
    second_shift,
    mode_mask,
    second_gain,
    second_bias,
    up_weight,
    up_bias,
    down_weight,
    down_bias,
):
    lats = lax.axis_size("lat")
    lons = lax.axis_size("lon")
    chs = lax.axis_size("ch")
    _, rows_here, cols_here, channels = grid_tokens.shape
    width = cols_here * lons
    height = rows_here * lats
    modes = width // 2
    modes_here = modes // lats
    part = channels // chs
    own = part // lons
    blocks_here = first_filter.shape[1] // lons
    ch_at = lax.axis_index("ch")
    lon_at = lax.axis_index("lon")
    steps = math.gcd(step_limit, rows_here // (lons * chs))
    line = rows_here // (lons * chs * steps)
    rows = chs * lons * line

    up_all = lax.all_gather(up_weight, "ch", axis=1, tiled=True)
    down_all = lax.all_gather(down_weight, "ch", axis=0, tiled=True)
    biases = lax.all_gather(jnp.concatenate([up_bias, down_bias]), "ch", axis=0, tiled=False)
    up_shift = biases[:, : up_bias.shape[0]].reshape(-1)
    down_shift = biases[:, up_bias.shape[0] :].reshape(-1)
    keep_mask = lax.all_gather(mode_mask, "lon", axis=1, tiled=True)

    tokens = grid_tokens[0]
    token_part = lax.dynamic_slice_in_dim(tokens, ch_at * part, part, 2)
    token_part = token_part.reshape(lons, chs, steps, line, cols_here, lons, own)
    arrived = []
    for step in range(steps):
        sent = jnp.transpose(token_part[:, :, step], (4, 3, 1, 0, 2, 5))
        sent = sent.reshape(lons, cols_here, rows * own)
        sent = lax.all_to_all(sent, "lon", split_axis=0, concat_axis=0, tiled=True)
        arrived.append(sent.reshape(width, rows, own))

    values = tokens.astype(jnp.float32)
    center = jnp.mean(values, axis=-1, keepdims=True)
    inv_dev = lax.rsqrt(
        jnp.mean(jnp.square(values - center), axis=-1, keepdims=True) + norm_epsilon
    )
    moments = jnp.stack([center[..., 0].T, inv_dev[..., 0].T])
    moments = lax.all_gather(moments, "lon", axis=1, tiled=True)
    moments = moments.reshape(2, width, lons, chs, steps, line)
    moments = jnp.transpose(moments, (4, 0, 1, 3, 2, 5)).reshape(steps, 2, width, rows, 1)
    own_at = ch_at * part + lon_at * own
    gain_part = lax.dynamic_slice_in_dim(first_gain, own_at, own, 0)
    bias_part = lax.dynamic_slice_in_dim(first_bias, own_at, own, 0)

    lon_forward, lon_inverse = lon_tables(width, modes)
    lat_forward, lat_inverse = lat_tables(height)
    shape = (2, 2, height, lats, lons, chs, steps, line)
    order = (6, 3, 1, 5, 4, 7, 0, 2)
    lat_forward = jnp.transpose(lat_forward.reshape(shape), order).reshape(
        steps, lats, 2, rows, 2, height
    )
    lat_inverse = jnp.swapaxes(lat_inverse, 2, 3).reshape(shape)
    lat_inverse = jnp.transpose(lat_inverse, (6, 3, 0, 5, 4, 7, 1, 2)).reshape(
        steps, lats, 2, rows, 2, height
    )
    lon_inverse = jnp.swapaxes(lon_inverse.reshape(2, lats, modes_here, width), 0, 1)

    base = []
    spectra = []
    for step in range(steps):
        token_rows = arrived[step].astype(jnp.float32)
        normed = (
            (token_rows - moments[step, 0]) * moments[step, 1] * gain_part + bias_part
        ).astype(jnp.bfloat16)
        base.append((arrived[step], normed))
        sent = jnp.einsum("pkw,whc->phkc", lon_forward, normed, preferred_element_type=jnp.float32)
        sent = sent.astype(jnp.bfloat16).reshape(2, rows, lats, modes_here, own)
        sent = jnp.transpose(sent, (2, 0, 1, 3, 4)).reshape(lats, 2 * rows, modes_here * own)
        sent = lax.all_to_all(sent, "lat", split_axis=0, concat_axis=0, tiled=True)
        spectra.append(sent)
    spectrum_rows = jnp.concatenate(spectra, axis=0).reshape(
        steps, lats, 2, rows, modes_here, own
    )
    spectrum = jnp.einsum(
        "jlphxq,jlphkc->xqkc", lat_forward, spectrum_rows, preferred_element_type=jnp.float32
    ).astype(jnp.bfloat16)
    pick = lambda array: lax.dynamic_slice_in_dim(array, lon_at * blocks_here, blocks_here, 1)
    filtered_modes = mode_mixer(
        spectrum[None],
        pick(first_filter),
        pick(first_shift),
        pick(second_filter),
        pick(second_shift),
        keep_mask,
    )[0]

    returned = []
    for step in range(steps):
        sent = jnp.einsum(
            "lyhxq,xqkc->lykhc",
            lat_inverse[step],
            filtered_modes,
            preferred_element_type=jnp.float32,
        )
        sent = sent.astype(jnp.bfloat16).reshape(lats, 2 * modes_here, rows * own)
        sent = lax.all_to_all(sent, "lat", split_axis=0, concat_axis=0, tiled=True)
        returned.append(sent.reshape(lats, 2, modes_here, rows, own))

    results = []
    for step in range(steps):
        filtered = jnp.einsum(
            "lykw,lykhc->hcw", lon_inverse, returned[step], preferred_element_type=jnp.float32
        )
        token_rows, normed = base[step]
        kept = token_rows.astype(jnp.float32) + normed.astype(jnp.float32)
        mixed = (jnp.transpose(kept, (1, 2, 0)) + filtered).astype(jnp.bfloat16)
        mixed = mixed.reshape(chs * lons, line * own, width)
        mixed = lax.all_to_all(mixed, ("ch", "lon"), split_axis=0, concat_axis=0, tiled=True)
        mixed = jnp.swapaxes(mixed.reshape(chs * lons, line, own, width), 0, 1)
        mixed = mixed.reshape(line, channels, width)
        all_channels = mixed.astype(jnp.float32)
        center_two = jnp.mean(all_channels, axis=1, keepdims=True)
        inv_two = lax.rsqrt(
            jnp.mean(jnp.square(all_channels - center_two), axis=1, keepdims=True) + norm_epsilon
        )
        normed_two = (
            (all_channels - center_two) * inv_two * second_gain[:, None] + second_bias[:, None]
        ).astype(jnp.bfloat16)
        hidden = jnp.einsum("icw,cj->iwj", normed_two, up_all, preferred_element_type=jnp.float32)
        hidden = gelu(hidden + up_shift).astype(jnp.bfloat16)
        total = jnp.einsum("iwj,jc->iwc", hidden, down_all, preferred_element_type=jnp.float32)
        total = total + down_shift + jnp.swapaxes(mixed, 1, 2).astype(jnp.float32)
        total = total.astype(jnp.bfloat16).reshape(line * width, chs, part)
        sent = jnp.swapaxes(total, 0, 1)
        sent = lax.all_to_all(sent, "ch", split_axis=0, concat_axis=0, tiled=True)
        results.append(sent.reshape(chs, line, width, part))
    return jnp.stack(results, axis=1).reshape(1, chs * steps * line, width, part)


def solution(mesh):
    in_specs = (
        P(None, "lat", "lon", None),
        P(),
        P(),
        P(None, "ch", None, None),
        P(None, "ch", None),
        P(None, "ch", None, None),
        P(None, "ch", None),
        P(None, ("lat", "lon")),
        P(),
        P(),
        P(None, "ch"),
        P("ch"),
        P("ch", None),
        P("ch"),
    )
    out_specs = P(None, ("lat", "lon"), None, "ch")
    blocks_here = block_total // mesh.shape["ch"]
    fits = blocks_here % mesh.shape["lon"] == 0
    shards = block_shards if fits else dense_shards
    return jax.shard_map(shards, mesh=mesh, in_specs=in_specs, out_specs=out_specs, check_vma=False)
```

```python
import math

import jax
import jax.numpy as jnp
from jax import lax
from jax.sharding import PartitionSpec as P

shrink_level = 0.01
norm_epsilon = 1e-05
step_limit = 4
lag = 2
block_total = 8


def lon_tables(lon_width, mode_count):
    frequency = jnp.arange(mode_count, dtype=jnp.int32)[:, None]
    position = jnp.arange(lon_width, dtype=jnp.int32)[None, :]
    phases = frequency * position % lon_width
    angles = phases.astype(jnp.float32) * (2.0 * math.pi / lon_width)
    norm_scale = 1.0 / math.sqrt(lon_width)
    forward = jnp.stack([jnp.cos(angles) * norm_scale, -jnp.sin(angles) * norm_scale]).astype(
        jnp.bfloat16
    )
    factor = jnp.where(frequency == 0, 1.0, 2.0) * norm_scale
    inverse = jnp.stack([jnp.cos(angles) * factor, -jnp.sin(angles) * factor]).astype(jnp.bfloat16)
    return (forward, inverse)


def lat_tables(lat_height):
    indices = jnp.arange(lat_height, dtype=jnp.int32)
    phases = indices[:, None] * indices[None, :] % lat_height
    angles = phases.astype(jnp.float32) * (2.0 * math.pi / lat_height)
    norm_scale = 1.0 / math.sqrt(lat_height)
    cosine = jnp.cos(angles) * norm_scale
    sine_table = jnp.sin(angles) * norm_scale
    forward = jnp.stack([jnp.stack([cosine, sine_table]), jnp.stack([-sine_table, cosine])]).astype(
        jnp.bfloat16
    )
    inverse = jnp.stack([jnp.stack([cosine, -sine_table]), jnp.stack([sine_table, cosine])]).astype(
        jnp.bfloat16
    )
    return (forward, inverse)


def complex_weight(weights):
    real_part, imag_part = (weights[0], weights[1])
    top_half = jnp.stack([real_part, imag_part], axis=2)
    low_half = jnp.stack([-imag_part, real_part], axis=2)
    return jnp.stack([top_half, low_half])


def mode_mixer(spectrum, weight_one, shift_one, weight_two, shift_two, keep_mask):
    samples, _, lat_freqs, lon_freqs, channel_count = spectrum.shape
    block_count = weight_one.shape[1]
    block_width = weight_one.shape[2]
    split_spec = spectrum.reshape(samples, 2, lat_freqs, lon_freqs, block_count, block_width)
    first_layer = jnp.einsum(
        "bpxyni,pniqo->bqxyno",
        split_spec,
        complex_weight(weight_one),
        preferred_element_type=jnp.float32,
    )
    first_layer = jnp.maximum(first_layer + shift_one[None, :, None, None, :, :], 0.0).astype(
        jnp.bfloat16
    )
    second_layer = jnp.einsum(
        "bpxyni,pniqo->bqxyno",
        first_layer,
        complex_weight(weight_two),
        preferred_element_type=jnp.float32,
    )
    second_layer = second_layer + shift_two[None, :, None, None, :, :]
    second_layer = second_layer - jnp.clip(second_layer, -shrink_level, shrink_level)
    second_layer = second_layer * keep_mask.astype(jnp.float32)[None, None, :, :, None, None]
    return second_layer.astype(jnp.bfloat16).reshape(
        samples, 2, lat_freqs, lon_freqs, channel_count
    )


def dense_shards(
    grid_tokens,
    first_gain,
    first_bias,
    first_filter,
    first_shift,
    second_filter,
    second_shift,
    mode_mask,
    second_gain,
    second_bias,
    up_weight,
    up_bias,
    down_weight,
    down_bias,
):
    lat_count = lax.axis_size("lat")
    lon_count = lax.axis_size("lon")
    ch_count = lax.axis_size("ch")
    samples, rows_here, cols_here, channel_count = grid_tokens.shape
    full_width = cols_here * lon_count
    full_height = rows_here * lat_count
    part_chans = channel_count // ch_count
    offset = lax.axis_index("ch") * part_chans
    spread_count = lat_count * lon_count
    modes_here = full_width // 2 // spread_count
    values = grid_tokens.astype(jnp.float32)
    center = jnp.mean(values, axis=-1, keepdims=True)
    inv_dev = lax.rsqrt(
        jnp.mean(jnp.square(values - center), axis=-1, keepdims=True) + norm_epsilon
    )
    token_part = lax.dynamic_slice_in_dim(grid_tokens, offset, part_chans, 3)
    gain_part = lax.dynamic_slice_in_dim(first_gain, offset, part_chans, 0)
    bias_part = lax.dynamic_slice_in_dim(first_bias, offset, part_chans, 0)
    token_rows = lax.all_to_all(token_part, "lon", split_axis=1, concat_axis=2, tiled=True)
    moments = lax.all_to_all(
        jnp.concatenate([center, inv_dev], axis=3), "lon", split_axis=1, concat_axis=2, tiled=True
    )
    normed_rows = (
        (token_rows.astype(jnp.float32) - moments[..., 0:1]) * moments[..., 1:2] * gain_part
        + bias_part
    ).astype(jnp.bfloat16)
    row_pairs = normed_rows.shape[1]
    lon_forward, lon_inverse = lon_tables(full_width, full_width // 2)
    lat_forward, lat_inverse = lat_tables(full_height)
    row_spectrum = jnp.einsum(
        "pkw,brwc->brpkc", lon_forward, normed_rows, preferred_element_type=jnp.float32
    ).astype(jnp.bfloat16)
    packed = row_spectrum.reshape(samples, 1, row_pairs, 2, spread_count, modes_here, part_chans)
    arrived = lax.all_to_all(packed, ("lat", "lon"), split_axis=4, concat_axis=1, tiled=True)
    spectrum_rows = arrived.reshape(samples, full_height, 2, modes_here, part_chans)
    spectrum = jnp.einsum(
        "qpxh,bhpyc->bqxyc", lat_forward, spectrum_rows, preferred_element_type=jnp.float32
    ).astype(jnp.bfloat16)
    filtered_modes = mode_mixer(
        spectrum, first_filter, first_shift, second_filter, second_shift, mode_mask
    )
    back_rows = jnp.einsum(
        "qphx,bpxyc->bhqyc", lat_inverse, filtered_modes, preferred_element_type=jnp.float32
    ).astype(jnp.bfloat16)
    packed_back = back_rows.reshape(samples, spread_count, row_pairs, 2, 1, modes_here, part_chans)
    returned = lax.all_to_all(packed_back, ("lat", "lon"), split_axis=1, concat_axis=4, tiled=True)
    row_modes = returned.reshape(samples, row_pairs, 2, full_width // 2, part_chans)
    filtered = jnp.einsum(
        "pkw,brpkc->brwc", lon_inverse, row_modes, preferred_element_type=jnp.float32
    )
    mixed = (token_rows.astype(jnp.float32) + normed_rows.astype(jnp.float32) + filtered).astype(
        jnp.bfloat16
    )
    all_channels = lax.all_gather(mixed, "ch", axis=3, tiled=True).astype(jnp.float32)
    center_two = jnp.mean(all_channels, axis=-1, keepdims=True)
    inv_two = lax.rsqrt(
        jnp.mean(jnp.square(all_channels - center_two), axis=-1, keepdims=True) + norm_epsilon
    )
    normed_two = ((all_channels - center_two) * inv_two * second_gain + second_bias).astype(
        jnp.bfloat16
    )
    tokens = normed_two.reshape(-1, channel_count)
    hidden = jnp.dot(tokens, up_weight, preferred_element_type=jnp.float32) + up_bias
    hidden = jax.nn.gelu(hidden, approximate=False).astype(jnp.bfloat16)
    partial_rows = jnp.dot(hidden, down_weight, preferred_element_type=jnp.float32).reshape(
        samples, row_pairs, full_width, channel_count
    )
    summed = lax.psum_scatter(
        partial_rows.astype(jnp.bfloat16), "ch", scatter_dimension=3, tiled=True
    ).astype(jnp.float32)
    return (mixed.astype(jnp.float32) + down_bias + summed).astype(jnp.bfloat16)


def gelu(values):
    return 0.5 * values * (1.0 + lax.erf(values * math.sqrt(0.5)))


def exchange(blocks, axis, dim=0):
    count = lax.axis_size(axis)
    here = lax.axis_index(axis)
    result = blocks
    for shift in range(1, count):
        target = lax.rem(here + shift, count)
        source = lax.rem(here + count - shift, count)
        pairs = [(place, (place + shift) % count) for place in range(count)]
        moved = lax.ppermute(lax.dynamic_slice_in_dim(blocks, target, 1, dim), axis, pairs)
        result = lax.dynamic_update_slice_in_dim(result, moved, source, dim)
    return result


def collect(block, axis):
    count = lax.axis_size(axis)
    here = lax.axis_index(axis)
    result = jnp.broadcast_to(block[None], (count,) + block.shape)
    for shift in range(1, count):
        source = lax.rem(here + count - shift, count)
        pairs = [(place, (place + shift) % count) for place in range(count)]
        moved = lax.ppermute(block, axis, pairs)
        result = lax.dynamic_update_slice_in_dim(result, moved[None], source, 0)
    return result


def block_shards(
    grid_tokens,
    first_gain,
    first_bias,
    first_filter,
    first_shift,
    second_filter,
    second_shift,
    mode_mask,
    second_gain,
    second_bias,
    up_weight,
    up_bias,
    down_weight,
    down_bias,
):
    lats = lax.axis_size("lat")
    lons = lax.axis_size("lon")
    chs = lax.axis_size("ch")
    _, rows_here, cols_here, channels = grid_tokens.shape
    width = cols_here * lons
    height = rows_here * lats
    modes = width // 2
    modes_here = modes // lats
    part = channels // chs
    own = part // lons
    blocks_here = first_filter.shape[1] // lons
    ch_at = lax.axis_index("ch")
    lon_at = lax.axis_index("lon")
    steps = math.gcd(step_limit, rows_here // (lons * chs))
    line = rows_here // (lons * chs * steps)
    rows = chs * lons * line

    tokens = grid_tokens[0]
    values = tokens.astype(jnp.float32)
    center = jnp.mean(values, axis=-1)
    inv_dev = lax.rsqrt(
        jnp.mean(jnp.square(values - center[..., None]), axis=-1) + norm_epsilon
    )
    moments = collect(jnp.stack([center, inv_dev]), "lon")
    moments = moments.reshape(lons, 2, lons, chs, steps, line, cols_here)
    moments = jnp.transpose(moments, (4, 1, 0, 2, 3, 5, 6)).reshape(
        steps, 2, lons, rows, cols_here, 1
    )
    token_part = lax.dynamic_slice_in_dim(tokens, ch_at * part, part, 2)
    token_part = token_part.reshape(lons, chs, steps, line, cols_here, part)
    ready = []
    for step in range(steps):
        step_rows = token_part[:, :, step]
        sent = jnp.stack(
            [
                step_rows[..., at * own : (at + 1) * own].reshape(rows, cols_here * own)
                for at in range(lons)
            ]
        )
        ready.append(sent)
    fetch = lambda sent: exchange(sent, "lon").reshape(lons, rows, cols_here, own)
    arrived = [fetch(sent) for sent in ready[:lag]]

    chs_pair = [(place, (place + 1) % chs) for place in range(chs)]
    beside = lambda array: lax.ppermute(array, "ch", chs_pair)
    own_at = ch_at * part + lon_at * own
    gain_part = lax.dynamic_slice_in_dim(first_gain, own_at, own, 0)
    bias_part = lax.dynamic_slice_in_dim(first_bias, own_at, own, 0)

    lon_forward, lon_inverse = lon_tables(width, modes)
    lat_forward, lat_inverse = lat_tables(height)
    shape = (2, 2, height, lats, lons, chs, steps, line)
    order = (6, 3, 1, 4, 5, 7, 0, 2)
    lat_forward = jnp.transpose(lat_forward.reshape(shape), order).reshape(
        steps, lats, 2, rows, 2, height
    )
    lat_inverse = jnp.swapaxes(lat_inverse, 2, 3).reshape(shape)
    lat_inverse = jnp.transpose(lat_inverse, (6, 3, 0, 4, 5, 7, 1, 2)).reshape(
        steps, lats, 2, rows, 2, height
    )
    lon_inverse = jnp.swapaxes(lon_inverse.reshape(2, lats, modes_here, width), 0, 1)

    lon_forward = lon_forward.reshape(2, modes, lons, cols_here)
    base = []
    spectra = []
    for step in range(steps):
        token_rows = arrived[step].astype(jnp.float32)
        normed = (
            (token_rows - moments[step, 0]) * moments[step, 1] * gain_part + bias_part
        ).astype(jnp.bfloat16)
        base.append((arrived[step], normed))
        sent = jnp.einsum("pkzw,zhwc->phkc", lon_forward, normed, preferred_element_type=jnp.float32)
        sent = sent.astype(jnp.bfloat16).reshape(2, rows, lats, modes_here, own)
        sent = jnp.transpose(sent, (2, 0, 1, 3, 4)).reshape(lats, 2 * rows, modes_here * own)
        if step == min(1, steps - 1):
            held = (sent, up_weight, down_weight, up_bias, down_bias, mode_mask)
            sent, up_sent, down_sent, up_bias_sent, down_bias_sent, mask_sent = (
                lax.optimization_barrier(held)
            )
            up_other, down_other = beside(up_sent), beside(down_sent)
            up_shift = jnp.concatenate([up_bias, beside(up_bias_sent)])
            down_shift = collect(down_bias_sent, "ch").reshape(-1)
            keep_mask = collect(mask_sent, "lon")
            keep_mask = jnp.swapaxes(keep_mask, 0, 1).reshape(height, modes_here)
        if step + lag < steps:
            sent, later = lax.optimization_barrier((sent, ready[step + lag]))
            arrived.append(fetch(later))
        spectra.append(exchange(sent, "lat"))
    up_all = jnp.concatenate([up_weight, up_other], axis=1)
    down_all = jnp.concatenate([down_weight, down_other], axis=0)
    spectrum_rows = jnp.concatenate(spectra, axis=0).reshape(
        steps, lats, 2, rows, modes_here, own
    )
    spectrum = jnp.einsum(
        "jlphxq,jlphkc->xqkc", lat_forward, spectrum_rows, preferred_element_type=jnp.float32
    ).astype(jnp.bfloat16)
    pick = lambda array: lax.dynamic_slice_in_dim(array, lon_at * blocks_here, blocks_here, 1)
    filtered_modes = mode_mixer(
        spectrum[None],
        pick(first_filter),
        pick(first_shift),
        pick(second_filter),
        pick(second_shift),
        keep_mask,
    )[0]

    def latitude_rows(step):
        sent = jnp.einsum(
            "lyhxq,xqkc->lykhc",
            lat_inverse[step],
            filtered_modes,
            preferred_element_type=jnp.float32,
        )
        return sent.astype(jnp.bfloat16).reshape(lats, 2 * modes_here, rows * own)

    def row_modes(sent):
        return exchange(sent, "lat").reshape(lats, 2, modes_here, rows, own)

    back_rows = [latitude_rows(step) for step in range(steps)]
    returned = [row_modes(sent) for sent in back_rows[:lag]]

    results = []
    totals = []

    def mixed_rows(step):
        filtered = jnp.einsum(
            "lykw,lykhc->hwc", lon_inverse, returned[step], preferred_element_type=jnp.float32
        )
        token_rows, normed = base[step]
        kept = token_rows.astype(jnp.float32) + normed.astype(jnp.float32)
        kept = jnp.swapaxes(kept, 0, 1).reshape(rows, width, own)
        mixed = (kept + filtered).astype(jnp.bfloat16)
        mixed = jnp.swapaxes(mixed, 1, 2).reshape(lons, chs, line * own, width)
        mixed = exchange(mixed, "ch", 1)
        if step + lag < steps:
            mixed, later = lax.optimization_barrier((mixed, back_rows[step + lag]))
            returned.append(row_modes(later))
        return mixed

    sent = mixed_rows(0)
    for step in range(steps):
        mixed = exchange(sent, "lon")
        if step + 1 < steps:
            sent = mixed_rows(step + 1)
            if step > 0:
                sent, _ = lax.optimization_barrier((sent, totals[step - 1]))
            mixed, _ = lax.optimization_barrier((mixed, sent))
        mixed = jnp.transpose(mixed.reshape(lons, chs, line, own, width), (2, 1, 0, 3, 4))
        mixed = mixed.reshape(line, channels, width)
        all_channels = mixed.astype(jnp.float32)
        center_two = jnp.mean(all_channels, axis=1, keepdims=True)
        inv_two = lax.rsqrt(
            jnp.mean(jnp.square(all_channels - center_two), axis=1, keepdims=True) + norm_epsilon
        )
        normed_two = (
            (all_channels - center_two) * inv_two * second_gain[:, None] + second_bias[:, None]
        ).astype(jnp.bfloat16)
        hidden = jnp.einsum("icw,cj->iwj", normed_two, up_all, preferred_element_type=jnp.float32)
        hidden = gelu(hidden + up_shift).astype(jnp.bfloat16)
        total = jnp.einsum("iwj,jc->iwc", hidden, down_all, preferred_element_type=jnp.float32)
        total = total + down_shift + jnp.swapaxes(mixed, 1, 2).astype(jnp.float32)
        total = total.astype(jnp.bfloat16).reshape(line * width, chs, part)
        totals.append(jnp.swapaxes(total, 0, 1))
    for total in totals:
        results.append(exchange(total, "ch").reshape(chs, line, width, part))
    return jnp.stack(results, axis=1).reshape(1, chs * steps * line, width, part)


def solution(mesh):
    in_specs = (
        P(None, "lat", "lon", None),
        P(),
        P(),
        P(None, "ch", None, None),
        P(None, "ch", None),
        P(None, "ch", None, None),
        P(None, "ch", None),
        P(None, ("lat", "lon")),
        P(),
        P(),
        P(None, "ch"),
        P("ch"),
        P("ch", None),
        P("ch"),
    )
    out_specs = P(None, ("lat", "lon"), None, "ch")
    lons, chs = mesh.shape["lon"], mesh.shape["ch"]
    fits = chs == 2 and block_total // chs % lons == 0
    shards = block_shards if fits else dense_shards
    return jax.shard_map(shards, mesh=mesh, in_specs=in_specs, out_specs=out_specs, check_vma=False)
```
